512 devices in a mesh: wide: 128 (over z, y, core), narrow: 4 (over x).
Axes of the slice: x: 4, y: 4, z: 16, core: 2. Of those that a mesh axis runs over, the one named last changes fastest.
Arguments:
- sketch: float32 [64, 65536], P(None, ('wide', 'narrow')), may hold values from -1000 to 1000
- ppmi_slab: float32 [4096, 65536], P('wide', 'narrow'), may hold values from 0 to 8
Outputs:
- orthonormal: float32 [64, 65536], P(None, ('wide', 'narrow'))
- projected: float32 [64, 65536], P(None, ('narrow', 'wide'))
The draws below stay inside these ranges and needn't reach their ends.
All inputs are finite; a program needn't handle non-finite values.
Results may differ from the reference program's by a relative error of at most 0.000076.
Values sent between devices are 32-bit elements; how exact they have to be, the bound alone decides.
No kernel may reach another device: no remote copies, remote signals or barrier semaphores. Data moves between devices by JAX's collectives and lax.ppermute only.
A program may use at most 64 MiB of HBM per device.

```python
import math
import jax
import jax.numpy as jnp
from jax import lax

K = 64
COLS = 65536
SK_DEV = 128
SUB = 8
ROWS = 65536
SLAB = 4096


def draw_sketch(key, part):
    key = jax.random.fold_in(key, 1)
    keys = jax.random.split(key, 3)
    width_scale = jnp.exp(jax.random.uniform(keys[0], (K, 1), jnp.float32) * 2.302585)
    row_scale = jnp.exp(jax.random.uniform(keys[1], (1, ROWS), jnp.float32) * 2.302585)
    base = jnp.clip(jax.random.normal(keys[2], (K, ROWS), jnp.float32), -5.0, 5.0)
    return width_scale * row_scale * base


def draw_ppmi_slab(key, part):
    key = jax.random.fold_in(key, 2)
    keys = jax.random.split(key, 1)
    base = jnp.clip(jax.random.normal(keys[0], (SLAB, COLS), jnp.float32), -5.0, 5.0)
    return jnp.maximum(1.5 * base - 0.4, 0.0)


def setup_inputs(seed: int = 0) -> dict:
    arg_keys = jax.random.split(jax.random.key(seed), 3)
    sketch = draw_sketch(jax.random.fold_in(arg_keys[2], 71), 0)
    ppmi_slab = draw_ppmi_slab(jax.random.fold_in(arg_keys[2], 71), 0)
    return {"sketch": sketch, "ppmi_slab": ppmi_slab}


def reference(sketch, ppmi_slab):
    gram_matrix = jnp.dot(sketch, sketch.T, precision=lax.Precision.HIGHEST) / ROWS
    lower_factor = jnp.linalg.cholesky(gram_matrix)
    orthonormal = lax.linalg.triangular_solve(lower_factor, sketch, left_side=True, lower=True)
    selected = orthonormal.reshape(K, ROWS // SK_DEV, SK_DEV)[:, :, :SUB].reshape(K, SLAB)
    projected = jnp.dot(selected, ppmi_slab, precision=lax.Precision.HIGHEST) * (1.0 / math.sqrt(SLAB))
    return (orthonormal, projected)
```

```python
import jax
import jax.numpy as jnp
from jax import lax
from jax.sharding import Mesh, PartitionSpec as P

SUB = 8
HI = lax.Precision.HIGHEST


def local(sketch, slab):
    k, sk = sketch.shape
    nz, ny, nc, nx = (lax.axis_size(a) for a in ("z", "y", "c", "x"))
    rows, cols = slab.shape
    out = cols // (nz * ny * nc)
    y, c = lax.axis_index("y"), lax.axis_index("c")
    blocks = slab.reshape(rows, nz, ny, nc * out)
    sent = []
    for d in range(ny):
        piece = lax.dynamic_index_in_dim(blocks, lax.rem(y + d, ny), 2, keepdims=False)
        if d:
            piece = lax.ppermute(piece, "y", [(i, (i + d) % ny) for i in range(ny)])
        sent.append(piece)

    gram = jnp.dot(sketch, sketch.T, precision=HI) / (sk * nz * ny * nc * nx)
    own = jnp.concatenate([sketch[:, :SUB].T, gram], axis=0)
    got = lax.all_to_all(jnp.broadcast_to(own, (nx, *own.shape)), "x", 0, 0, tiled=True)
    sel = got[:, :SUB].reshape(nx * SUB, k)
    own = jnp.concatenate([sel, got[:, SUB:].sum(0)], axis=0)
    got = lax.all_to_all(jnp.broadcast_to(own, (ny * nc, *own.shape)), ("y", "c"), 0, 0, tiled=True)
    sel = got[:, :rows].reshape(ny, nc, rows, k)
    gram = got[:, rows:].sum(0)

    sel = lax.dynamic_index_in_dim(sel, c, 1, keepdims=False)
    part = 0.0
    for d in range(ny):
        s = lax.dynamic_index_in_dim(sel, lax.rem(y - d + ny, ny), 0, keepdims=False)
        part += lax.dot_general(s, sent[d].reshape(rows, nz * nc * out), (((0,), (0,)), ((), ())), precision=HI)
    part = part.reshape(k, nz, nc, out)
    keep = lax.dynamic_index_in_dim(part, c, 2, keepdims=False)
    away = lax.dynamic_index_in_dim(part, 1 - c, 2, keepdims=False)
    part = keep + lax.ppermute(away, "c", [(0, 1), (1, 0)])

    part = part.transpose(1, 0, 2)
    gram = jnp.broadcast_to(gram.reshape(-1, out), (nz, k * k // out, out))
    got = lax.all_to_all(jnp.concatenate([part, gram], axis=1), "z", 0, 0, tiled=True).sum(0)
    gram = got[k:].reshape(k, k)
    lower = jnp.linalg.cholesky(gram)
    both = jnp.concatenate([sketch, got[:k]], axis=1)
    both = lax.linalg.triangular_solve(lower, both, left_side=True, lower=True)
    total = rows * nz * ny * nc
    return both[:, :sk], both[:, sk:] * (1.0 / total**0.5)


def solution(mesh):
    nx = mesh.shape["narrow"]
    grid = Mesh(mesh.devices.reshape(-1, 4, 2, nx), ("z", "y", "c", "x"))
    return jax.shard_map(
        local,
        mesh=grid,
        in_specs=(P(None, ("z", "y", "c", "x")), P(("z", "y", "c"), "x")),
        out_specs=(P(None, ("z", "y", "c", "x")), P(None, ("x", "z", "y", "c"))),
        check_vma=False,
    )
```

```python
import functools

import jax
import jax.numpy as jnp
from jax import lax
from jax.experimental import pallas as pl
from jax.experimental.pallas import tpu as pltpu
from jax.sharding import Mesh, PartitionSpec as P

SUB = 8
HI = lax.Precision.HIGHEST
VMEM = pl.BlockSpec(memory_space=pltpu.VMEM)
BIG = pltpu.CompilerParams(vmem_limit_bytes=32 * 2**20)
F32 = jnp.float32


def pack_body(scale, s_ref, o_ref):
    s = s_ref[...]
    k = s.shape[0]
    n = o_ref.shape[0]
    half = k // 2
    gram = lax.dot_general(s, s, (((1,), (1,)), ((), ())), precision=HI, preferred_element_type=F32) * scale
    gram = jnp.concatenate([gram[:half], gram[half:]], axis=1)
    sel = s.T[:SUB]
    sel = jnp.concatenate([sel, jnp.zeros_like(sel)], axis=1)
    o_ref[...] = jnp.broadcast_to(jnp.concatenate([gram, sel], axis=0)[None], o_ref.shape)


def sort_body(x_ref, t_ref, o_ref):
    ng = o_ref.shape[0]
    rows, cols = x_ref.shape
    nx, _, w = t_ref.shape
    k = w // 2
    half = k // 2
    nh = cols // (ng * w)
    gl = ng // 2
    for zl in range(2):
        for j in range(gl):
            for zh in range(nh):
                at = ((zh * 2 + zl) * gl + j) * w
                o_ref[zl * gl + j, zh * rows : (zh + 1) * rows] = x_ref[:, at : at + w]
    sel = [t_ref[x, half:, :k] for x in range(nx)]
    sel = jnp.concatenate([jnp.concatenate(sel[: nx // 2], axis=0), jnp.concatenate(sel[nx // 2 :], axis=0)], axis=1)
    gram = jnp.sum(t_ref[:, :half], axis=0)
    tail = jnp.concatenate([sel, gram], axis=0)
    o_ref[:, nh * rows :] = jnp.broadcast_to(tail[None], (ng, *tail.shape))


def project_body(rows, t_ref, o_ref):
    ng = t_ref.shape[0]
    nh, tall, w = o_ref.shape
    k = w // 2
    at = nh * rows
    sel = [t_ref[g, at : at + rows // 2, h * k : (h + 1) * k] for g in range(ng) for h in range(2)]
    sel = jnp.concatenate(sel, axis=0)
    step = 2
    for z0 in range(0, nh, step):
        wide = [jnp.concatenate([t_ref[g, z * rows : (z + 1) * rows] for g in range(ng)], axis=0) for z in range(z0, z0 + step)]
        res = lax.dot_general(
            sel, jnp.concatenate(wide, axis=1), (((0,), (0,)), ((), ())), precision=HI, preferred_element_type=F32
        )
        for z in range(step):
            o_ref[z0 + z, :k] = res[:, z * w : (z + 1) * w]
    gram = jnp.sum(t_ref[:, at + rows // 2 :], axis=0)
    o_ref[:, k:] = jnp.broadcast_to(gram[None], (nh, tall - k, w))


def finish_body(scale, s_ref, t_ref, q_ref, p_ref):
    k = s_ref.shape[0]
    total = jnp.sum(t_ref[...], axis=0)
    eye = (lax.broadcasted_iota(jnp.int32, (k, k), 0) == lax.broadcasted_iota(jnp.int32, (k, k), 1)).astype(F32)
    gram = jnp.concatenate([total[k:, :k], total[k:, k:]], axis=0)
    m = jnp.concatenate([gram, eye], axis=1)
    row_of = lax.broadcasted_iota(jnp.int32, (k, 1), 0)
    for i in range(k - 1):
        factor = jnp.where(row_of > i, m[:, i : i + 1], 0.0) * (1.0 / m[i : i + 1, i : i + 1])
        m = m - factor * m[i : i + 1, :]
    pivots = jnp.sum(m[:, :k] * eye, axis=1, keepdims=True)
    inv = m[:, k:] * (1.0 / jnp.sqrt(pivots))
    q_ref[...] = jnp.dot(inv, s_ref[...], precision=HI, preferred_element_type=F32)
    p_ref[...] = jnp.dot(inv, total[:k], precision=HI, preferred_element_type=F32) * scale


def call(body, outs, name, *args):
    shapes = [jax.ShapeDtypeStruct(s, F32) for s in outs]
    return pl.pallas_call(
        body, out_shape=shapes, in_specs=[VMEM] * len(args), out_specs=[VMEM] * len(outs), compiler_params=BIG, name=name
    )(*args)


def local(sketch, slab):
    k, sk = sketch.shape
    nh, nl, ny, nc, nx = (lax.axis_size(a) for a in ("zh", "zl", "y", "c", "x"))
    rows, cols = slab.shape
    ng = nl * ny * nc
    out = cols // (nh * ng)
    half = k // 2

    (own,) = call(functools.partial(pack_body, 1.0 / (sk * nh * ng * nx)), [(nx, half + SUB, out)], "pack", sketch)
    own = lax.all_to_all(own, "x", 0, 0, tiled=True)
    (sent,) = call(sort_body, [(ng, nh * rows + rows // 2 + half, out)], "sort", slab, own)
    sent = lax.all_to_all(sent, ("zl", "y", "c"), 0, 0, tiled=True)
    (part,) = call(functools.partial(project_body, rows), [(nh, k + half, out)], "project", sent)
    part = lax.all_to_all(part, "zh", 0, 0, tiled=True)
    scale = 1.0 / (rows * nh * ng) ** 0.5
    ortho, projected = call(functools.partial(finish_body, scale), [(k, sk), (k, out)], "finish", sketch, part)
    return ortho, projected


def solution(mesh):
    nx = mesh.shape["narrow"]
    grid = Mesh(mesh.devices.reshape(-1, 2, 4, 2, nx), ("zh", "zl", "y", "c", "x"))
    wide = ("zh", "zl", "y", "c")
    return jax.shard_map(
        local,
        mesh=grid,
        in_specs=(P(None, (*wide, "x")), P(wide, "x")),
        out_specs=(P(None, (*wide, "x")), P(None, ("x", *wide))),
        check_vma=False,
    )
```

```python
import functools

import jax
import jax.numpy as jnp
from jax import lax
from jax.experimental import pallas as pl
from jax.experimental.pallas import tpu as pltpu
from jax.sharding import Mesh, PartitionSpec as P

SUB = 8
HI = lax.Precision.HIGHEST
SMEM = pl.BlockSpec(memory_space=pltpu.SMEM)
VMEM = pl.BlockSpec(memory_space=pltpu.VMEM)
BIG = pltpu.CompilerParams(vmem_limit_bytes=32 * 2**20)
F32 = jnp.float32


def pack_body(scale, s_ref, o_ref):
    s = s_ref[...]
    k = s.shape[0]
    half = k // 2
    gram = lax.dot_general(s, s, (((1,), (1,)), ((), ())), precision=HI, preferred_element_type=F32) * scale
    gram = jnp.concatenate([gram[:half], gram[half:]], axis=1)
    sel = s.T[:SUB]
    sel = jnp.concatenate([sel, jnp.zeros_like(sel)], axis=1)
    o_ref[...] = jnp.broadcast_to(jnp.concatenate([gram, sel], axis=0)[None], o_ref.shape)


def away_body(w, at_ref, x_ref, o_ref):
    for b in range(o_ref.shape[1] // w):
        col = pl.multiple_of((2 * b + 1 - at_ref[0]) * w, w)
        o_ref[:, b * w : (b + 1) * w] = x_ref[:, pl.ds(col, w)]


def sort_body(ny, at_ref, x_ref, a_ref, t_ref, o_ref):
    ng = o_ref.shape[0]
    rows = x_ref.shape[0]
    _, tall, w = t_ref.shape
    nh = a_ref.shape[1] // (ng * w)
    k = w // 2
    half = k // 2
    c = at_ref[0]
    mine = pl.multiple_of(c * rows, rows)
    other = pl.multiple_of((1 - c) * rows, rows)
    for g in range(ng):
        for zh in range(nh):
            b = (zh * 2 + g // ny) * ny + g % ny
            base = zh * 2 * rows
            o_ref[g, pl.ds(base + mine, rows)] = x_ref[:, pl.ds(pl.multiple_of((2 * b + c) * w, w), w)]
            o_ref[g, pl.ds(base + other, rows)] = a_ref[:, b * w : (b + 1) * w]
    n = t_ref.shape[0]
    sel = [t_ref[p, half:, :k] for p in range(n)]
    sel = jnp.concatenate([jnp.concatenate(sel[: n // 2], axis=0), jnp.concatenate(sel[n // 2 :], axis=0)], axis=1)
    gram = jnp.sum(t_ref[:, :half], axis=0)
    tail = jnp.concatenate([sel, gram], axis=0)
    o_ref[:, nh * 2 * rows :] = jnp.broadcast_to(tail[None], (ng, *tail.shape))


def project_body(rows, t_ref, o_ref):
    ng = t_ref.shape[0]
    nh, tall, w = o_ref.shape
    k = w // 2
    at = nh * rows
    sel = [t_ref[g, at : at + rows // 2, h * k : (h + 1) * k] for g in range(ng) for h in range(2)]
    sel = jnp.concatenate(sel, axis=0)
    step = 2
    for z0 in range(0, nh, step):
        wide = [jnp.concatenate([t_ref[g, z * rows : (z + 1) * rows] for g in range(ng)], axis=0) for z in range(z0, z0 + step)]
        res = lax.dot_general(
            sel, jnp.concatenate(wide, axis=1), (((0,), (0,)), ((), ())), precision=HI, preferred_element_type=F32
        )
        for z in range(step):
            o_ref[z0 + z, :k] = res[:, z * w : (z + 1) * w]
    gram = jnp.sum(t_ref[:, at + rows // 2 :], axis=0)
    o_ref[:, k:] = jnp.broadcast_to(gram[None], (nh, tall - k, w))


def inverse_factor(gram):
    k = gram.shape[0]
    eye = (lax.broadcasted_iota(jnp.int32, (k, k), 0) == lax.broadcasted_iota(jnp.int32, (k, k), 1)).astype(F32)
    m = jnp.concatenate([gram, eye], axis=1).reshape(k // SUB, SUB, 2 * k)
    tile = (SUB, 2 * k)
    row_of = lax.broadcasted_iota(jnp.int32, m.shape, 0) * SUB + lax.broadcasted_iota(jnp.int32, m.shape, 1)
    step = 4
    for i in range(0, k, step):
        js = range(step)
        rows = [jnp.broadcast_to(m[(i + j) // SUB, (i + j) % SUB : (i + j) % SUB + 1], tile) for j in js]
        cols = [jnp.broadcast_to(m[:, :, i + j : i + j + 1], m.shape) for j in js]
        piv = [[jnp.broadcast_to(rows[j][:, i + q : i + q + 1], tile) if q >= j else None for q in js] for j in js]
        for j in js:
            inv = 1.0 / piv[j][j]
            for q in range(j + 1, step):
                f = piv[j][q] * inv
                rows[q] = rows[q] - f * rows[j]
                cols[q] = cols[q] - f[None] * cols[j]
                for r in range(q, step):
                    piv[q][r] = piv[q][r] - f * piv[j][r]
            m = m - jnp.where(row_of > i + j, cols[j], 0.0) * (inv * rows[j])[None]
    m = m.reshape(k, 2 * k)
    pivots = jnp.sum(m[:, :k] * eye, axis=1, keepdims=True)
    return m[:, k:] * (1.0 / jnp.sqrt(pivots))


def finish_body(scale, s_ref, t_ref, q_ref, p_ref):
    k, sk = s_ref.shape
    total = jnp.sum(t_ref[...], axis=0)
    inv = inverse_factor(jnp.concatenate([total[k:, :k], total[k:, k:]], axis=0))
    both = jnp.concatenate([s_ref[...], total[:k] * scale], axis=1)
    both = jnp.dot(inv, both, precision=HI, preferred_element_type=F32)
    q_ref[...] = both[:, :sk]
    p_ref[...] = both[:, sk:]


def call(body, outs, name, *args):
    shapes = [jax.ShapeDtypeStruct(s, F32) for s in outs]
    where = [SMEM if a.ndim == 1 else VMEM for a in args]
    return pl.pallas_call(
        body, out_shape=shapes, in_specs=where, out_specs=[VMEM] * len(outs), compiler_params=BIG, name=name
    )(*args)


def local(sketch, slab):
    k, sk = sketch.shape
    nh, nl, ny, nc, nx = (lax.axis_size(a) for a in ("zh", "zl", "y", "c", "x"))
    rows, cols = slab.shape
    ng = nl * ny
    out = cols // (nh * ng * nc)
    half = k // 2
    at = lax.axis_index("c").astype(jnp.int32)[None]

    (own,) = call(functools.partial(pack_body, 1.0 / (sk * nh * ng * nc * nx)), [(nc * nx, half + SUB, out)], "pack", sketch)
    own = lax.all_to_all(own, ("c", "x"), 0, 0, tiled=True)
    (away,) = call(functools.partial(away_body, out), [(rows, cols // nc)], "away", at, slab)
    away = lax.ppermute(away, "c", [(0, 1), (1, 0)])
    rows *= nc
    (sent,) = call(functools.partial(sort_body, ny), [(ng, nh * rows + rows // 2 + half, out)], "sort", at, slab, away, own)
    sent = lax.all_to_all(sent, ("zl", "y"), 0, 0, tiled=True)
    (part,) = call(functools.partial(project_body, rows), [(nh, k + half, out)], "project", sent)
    part = lax.all_to_all(part, "zh", 0, 0, tiled=True)
    scale = 1.0 / (rows * nh * ng) ** 0.5
    ortho, projected = call(functools.partial(finish_body, scale), [(k, sk), (k, out)], "finish", sketch, part)
    return ortho, projected


def solution(mesh):
    nx = mesh.shape["narrow"]
    grid = Mesh(mesh.devices.reshape(-1, 2, 4, 2, nx), ("zh", "zl", "y", "c", "x"))
    wide = ("zh", "zl", "y", "c")
    return jax.shard_map(
        local,
        mesh=grid,
        in_specs=(P(None, (*wide, "x")), P(wide, "x")),
        out_specs=(P(None, (*wide, "x")), P(None, ("x", *wide))),
        check_vma=False,
    )
```

```python
import functools

import jax
import jax.numpy as jnp
from jax import lax
from jax.experimental import pallas as pl
from jax.experimental.pallas import tpu as pltpu
from jax.sharding import Mesh, PartitionSpec as P

SUB = 8
HI = lax.Precision.HIGHEST
SMEM = pl.BlockSpec(memory_space=pltpu.SMEM)
VMEM = pl.BlockSpec(memory_space=pltpu.VMEM)
BIG = pltpu.CompilerParams(vmem_limit_bytes=32 * 2**20)
F32 = jnp.float32


GRAM = 24


def fold(gram):
    k = gram.shape[0]
    h, q = k // 2, k // 4
    a, b, c = gram[:h, :h], gram[:h, h:], gram[h:, h:]
    row, col = (lax.broadcasted_iota(jnp.int32, (h, h), d) for d in (0, 1))
    both = jnp.concatenate([jnp.where(row > col, a, c), b], axis=1)
    both = jnp.concatenate([both[:q], both[q:]], axis=1)
    diag = jnp.sum(jnp.where(row == col, a, 0.0), axis=0, keepdims=True)
    diag = jnp.concatenate([diag, jnp.zeros((1, 2 * k - h), F32)], axis=1)
    return jnp.concatenate([both, diag, jnp.zeros((GRAM - q - 1, 2 * k), F32)], axis=0)


def unfold(tile):
    k = tile.shape[1] // 2
    h, q = k // 2, k // 4
    both = jnp.concatenate([tile[:q, :k], tile[:q, k:]], axis=0)
    turned = both.T
    row, col = (lax.broadcasted_iota(jnp.int32, (h, h), d) for d in (0, 1))
    x, xt = both[:, :h], turned[:h]
    diag = jnp.broadcast_to(tile[q : q + 1, :h], (h, h))
    a = jnp.where(row > col, x, jnp.where(row < col, xt, diag))
    c = jnp.where(row <= col, x, xt)
    return jnp.concatenate(
        [jnp.concatenate([a, both[:, h:]], axis=1), jnp.concatenate([turned[h:], c], axis=1)], axis=0
    )


def pack_body(scale, s_ref, o_ref):
    s = s_ref[...]
    gram = lax.dot_general(s, s, (((1,), (1,)), ((), ())), precision=HI, preferred_element_type=F32) * scale
    sel = s.T[:SUB]
    sel = jnp.concatenate([sel, jnp.zeros_like(sel)], axis=1)
    o_ref[...] = jnp.broadcast_to(jnp.concatenate([fold(gram), sel], axis=0)[None], o_ref.shape)


def away_body(w, at_ref, x_ref, o_ref):
    for b in range(o_ref.shape[1] // w):
        col = pl.multiple_of((2 * b + 1 - at_ref[0]) * w, w)
        o_ref[:, b * w : (b + 1) * w] = x_ref[:, pl.ds(col, w)]


def sort_body(ny, at_ref, x_ref, a_ref, t_ref, o_ref):
    ng = o_ref.shape[0]
    rows = x_ref.shape[0]
    _, tall, w = t_ref.shape
    nh = a_ref.shape[1] // (ng * w)
    k = w // 2
    half = tall - SUB
    c = at_ref[0]
    mine = pl.multiple_of(c * rows, rows)
    other = pl.multiple_of((1 - c) * rows, rows)
    for g in range(ng):
        for zh in range(nh):
            b = (zh * 2 + g // ny) * ny + g % ny
            base = zh * 2 * rows
            o_ref[g, pl.ds(base + mine, rows)] = x_ref[:, pl.ds(pl.multiple_of((2 * b + c) * w, w), w)]
            o_ref[g, pl.ds(base + other, rows)] = a_ref[:, b * w : (b + 1) * w]
    n = t_ref.shape[0]
    sel = [t_ref[p, half:, :k] for p in range(n)]
    sel = jnp.concatenate([jnp.concatenate(sel[: n // 2], axis=0), jnp.concatenate(sel[n // 2 :], axis=0)], axis=1)
    gram = jnp.sum(t_ref[:, :half], axis=0)
    tail = jnp.concatenate([sel, gram], axis=0)
    o_ref[:, nh * 2 * rows :] = jnp.broadcast_to(tail[None], (ng, *tail.shape))


def project_body(rows, t_ref, o_ref):
    ng = t_ref.shape[0]
    nh, tall, w = o_ref.shape
    k = w // 2
    at = nh * rows
    sel = [t_ref[g, at : at + rows // 2, h * k : (h + 1) * k] for g in range(ng) for h in range(2)]
    sel = jnp.concatenate(sel, axis=0)
    step = 2
    for z0 in range(0, nh, step):
        wide = [jnp.concatenate([t_ref[g, z * rows : (z + 1) * rows] for g in range(ng)], axis=0) for z in range(z0, z0 + step)]
        res = lax.dot_general(
            sel, jnp.concatenate(wide, axis=1), (((0,), (0,)), ((), ())), precision=HI, preferred_element_type=F32
        )
        for z in range(step):
            o_ref[z0 + z, :k] = res[:, z * w : (z + 1) * w]
    gram = jnp.sum(t_ref[:, at + rows // 2 :], axis=0)
    o_ref[:, k:] = jnp.broadcast_to(gram[None], (nh, tall - k, w))


def inverse_factor(gram):
    k = gram.shape[0]
    eye = (lax.broadcasted_iota(jnp.int32, (k, k), 0) == lax.broadcasted_iota(jnp.int32, (k, k), 1)).astype(F32)
    m = jnp.concatenate([gram, eye], axis=1).reshape(k // SUB, SUB, 2 * k)
    tile = (SUB, 2 * k)
    row_of = lax.broadcasted_iota(jnp.int32, m.shape, 0) * SUB + lax.broadcasted_iota(jnp.int32, m.shape, 1)
    step = SUB
    for i in range(0, k, step):
        js = range(step)
        rows = [jnp.broadcast_to(m[(i + j) // SUB, (i + j) % SUB : (i + j) % SUB + 1], tile) for j in js]
        cols = [jnp.broadcast_to(m[:, :, i + j : i + j + 1], m.shape) for j in js]
        piv = [[jnp.broadcast_to(rows[j][:, i + q : i + q + 1], tile) if q >= j else None for q in js] for j in js]
        for j in js:
            inv = 1.0 / piv[j][j]
            for q in range(j + 1, step):
                f = piv[j][q] * inv
                rows[q] = rows[q] - f * rows[j]
                cols[q] = cols[q] - f[None] * cols[j]
                for r in range(q, step):
                    piv[q][r] = piv[q][r] - f * piv[j][r]
            m = m - jnp.where(row_of > i + j, cols[j], 0.0) * (inv * rows[j])[None]
    m = m.reshape(k, 2 * k)
    pivots = jnp.sum(m[:, :k] * eye, axis=1, keepdims=True)
    return m[:, k:] * (1.0 / jnp.sqrt(pivots))


def finish_body(scale, s_ref, t_ref, q_ref, p_ref):
    k, sk = s_ref.shape
    total = jnp.sum(t_ref[...], axis=0)
    inv = inverse_factor(unfold(total[k:]))
    both = jnp.concatenate([s_ref[...], total[:k] * scale], axis=1)
    both = jnp.dot(inv, both, precision=HI, preferred_element_type=F32)
    q_ref[...] = both[:, :sk]
    p_ref[...] = both[:, sk:]


def call(body, outs, name, *args):
    shapes = [jax.ShapeDtypeStruct(s, F32) for s in outs]
    where = [SMEM if a.ndim == 1 else VMEM for a in args]
    return pl.pallas_call(
        body, out_shape=shapes, in_specs=where, out_specs=[VMEM] * len(outs), compiler_params=BIG, name=name
    )(*args)


def local(sketch, slab):
    k, sk = sketch.shape
    nh, nl, ny, nc, nx = (lax.axis_size(a) for a in ("zh", "zl", "y", "c", "x"))
    rows, cols = slab.shape
    ng = nl * ny
    out = cols // (nh * ng * nc)
    at = lax.axis_index("c").astype(jnp.int32)[None]

    (own,) = call(functools.partial(pack_body, 1.0 / (sk * nh * ng * nc * nx)), [(nc * nx, GRAM + SUB, out)], "pack", sketch)
    own = lax.all_to_all(own, ("c", "x"), 0, 0, tiled=True)
    (away,) = call(functools.partial(away_body, out), [(rows, cols // nc)], "away", at, slab)
    away = lax.ppermute(away, "c", [(0, 1), (1, 0)])
    rows *= nc
    (sent,) = call(functools.partial(sort_body, ny), [(ng, nh * rows + rows // 2 + GRAM, out)], "sort", at, slab, away, own)
    sent = lax.all_to_all(sent, ("zl", "y"), 0, 0, tiled=True)
    (part,) = call(functools.partial(project_body, rows), [(nh, k + GRAM, out)], "project", sent)
    part = lax.all_to_all(part, "zh", 0, 0, tiled=True)
    scale = 1.0 / (rows * nh * ng) ** 0.5
    ortho, projected = call(functools.partial(finish_body, scale), [(k, sk), (k, out)], "finish", sketch, part)
    return ortho, projected


def solution(mesh):
    nx = mesh.shape["narrow"]
    grid = Mesh(mesh.devices.reshape(-1, 2, 4, 2, nx), ("zh", "zl", "y", "c", "x"))
    wide = ("zh", "zl", "y", "c")
    return jax.shard_map(
        local,
        mesh=grid,
        in_specs=(P(None, (*wide, "x")), P(wide, "x")),
        out_specs=(P(None, (*wide, "x")), P(None, ("x", *wide))),
        check_vma=False,
    )
```

```python
import functools

import jax
import jax.numpy as jnp
from jax import lax
from jax.experimental import pallas as pl
from jax.experimental.pallas import tpu as pltpu
from jax.sharding import Mesh, PartitionSpec as P

SUB = 8
HI = lax.Precision.HIGHEST
SMEM = pl.BlockSpec(memory_space=pltpu.SMEM)
VMEM = pl.BlockSpec(memory_space=pltpu.VMEM)
BIG = pltpu.CompilerParams(vmem_limit_bytes=32 * 2**20)
F32 = jnp.float32
PLACE = (0, 4, 2, 6, 1, 5, 3, 7)


GRAM = 24


def fold(gram):
    k = gram.shape[0]
    h, q = k // 2, k // 4
    a, b, c = gram[:h, :h], gram[:h, h:], gram[h:, h:]
    row, col = (lax.broadcasted_iota(jnp.int32, (h, h), d) for d in (0, 1))
    both = jnp.concatenate([jnp.where(row > col, a, c), b], axis=1)
    both = jnp.concatenate([both[:q], both[q:]], axis=1)
    diag = jnp.sum(jnp.where(row == col, a, 0.0), axis=0, keepdims=True)
    diag = jnp.concatenate([diag, jnp.zeros((1, 2 * k - h), F32)], axis=1)
    return jnp.concatenate([both, diag, jnp.zeros((GRAM - q - 1, 2 * k), F32)], axis=0)


def unfold(tile):
    k = tile.shape[1] // 2
    h, q = k // 2, k // 4
    both = jnp.concatenate([tile[:q, :k], tile[:q, k:]], axis=0)
    turned = both.T
    row, col = (lax.broadcasted_iota(jnp.int32, (h, h), d) for d in (0, 1))
    x, xt = both[:, :h], turned[:h]
    diag = jnp.broadcast_to(tile[q : q + 1, :h], (h, h))
    a = jnp.where(row > col, x, jnp.where(row < col, xt, diag))
    c = jnp.where(row <= col, x, xt)
    return jnp.concatenate(
        [jnp.concatenate([a, both[:, h:]], axis=1), jnp.concatenate([turned[h:], c], axis=1)], axis=0
    )


def pack_body(scale, s_ref, o_ref):
    s = s_ref[...]
    gram = lax.dot_general(s, s, (((1,), (1,)), ((), ())), precision=HI, preferred_element_type=F32) * scale
    sel = s.T[:SUB]
    sel = jnp.concatenate([sel, jnp.zeros_like(sel)], axis=1)
    o_ref[...] = jnp.broadcast_to(jnp.concatenate([fold(gram), sel], axis=0)[None], o_ref.shape)


def away_body(w, at_ref, x_ref, o_ref):
    for b in range(o_ref.shape[1] // w):
        col = pl.multiple_of((2 * b + 1 - at_ref[0]) * w, w)
        o_ref[:, b * w : (b + 1) * w] = x_ref[:, pl.ds(col, w)]


def sort_body(ny, at_ref, x_ref, a_ref, t_ref, o_ref):
    ng = o_ref.shape[0]
    rows = x_ref.shape[0]
    _, tall, w = t_ref.shape
    nh = a_ref.shape[1] // (ng * w)
    k = w // 2
    half = tall - SUB
    c = at_ref[0]
    mine = pl.multiple_of(c * rows, rows)
    other = pl.multiple_of((1 - c) * rows, rows)
    for g in range(ng):
        for zh in range(nh):
            b = (zh * 2 + g // ny) * ny + g % ny
            base = zh * 2 * rows
            o_ref[g, pl.ds(base + mine, rows)] = x_ref[:, pl.ds(pl.multiple_of((2 * b + c) * w, w), w)]
            o_ref[g, pl.ds(base + other, rows)] = a_ref[:, b * w : (b + 1) * w]
    n = t_ref.shape[0]
    sel = [t_ref[p, half:, :k] for p in range(n)]
    sel = jnp.concatenate([jnp.concatenate(sel[: n // 2], axis=0), jnp.concatenate(sel[n // 2 :], axis=0)], axis=1)
    gram = jnp.sum(t_ref[:, :half], axis=0)
    tail = jnp.concatenate([sel, gram], axis=0)
    o_ref[:, nh * 2 * rows :] = jnp.broadcast_to(tail[None], (ng, *tail.shape))


def project_body(rows, t_ref, o_ref):
    ng = t_ref.shape[0]
    nh, tall, w = o_ref.shape
    k = w // 2
    at = nh * rows
    sel = [t_ref[g, at : at + rows // 2, h * k : (h + 1) * k] for g in range(ng) for h in range(2)]
    sel = jnp.concatenate(sel, axis=0)
    step = 2
    for z0 in range(0, nh, step):
        wide = [jnp.concatenate([t_ref[g, z * rows : (z + 1) * rows] for g in range(ng)], axis=0) for z in range(z0, z0 + step)]
        res = lax.dot_general(
            sel, jnp.concatenate(wide, axis=1), (((0,), (0,)), ((), ())), precision=HI, preferred_element_type=F32
        )
        for z in range(step):
            o_ref[PLACE[z0 + z], :k] = res[:, z * w : (z + 1) * w]
    gram = jnp.sum(t_ref[:, at + rows // 2 :], axis=0)
    o_ref[:, k:] = jnp.broadcast_to(gram[None], (nh, tall - k, w))


def inverse_factor(gram):
    k = gram.shape[0]
    eye = (lax.broadcasted_iota(jnp.int32, (k, k), 0) == lax.broadcasted_iota(jnp.int32, (k, k), 1)).astype(F32)
    m = jnp.concatenate([gram, eye], axis=1).reshape(k // SUB, SUB, 2 * k)
    tile = (SUB, 2 * k)
    row_of = lax.broadcasted_iota(jnp.int32, m.shape, 0) * SUB + lax.broadcasted_iota(jnp.int32, m.shape, 1)
    step = SUB
    for i in range(0, k, step):
        js = range(step)
        rows = [jnp.broadcast_to(m[(i + j) // SUB, (i + j) % SUB : (i + j) % SUB + 1], tile) for j in js]
        cols = [jnp.broadcast_to(m[:, :, i + j : i + j + 1], m.shape) for j in js]
        piv = [[jnp.broadcast_to(rows[j][:, i + q : i + q + 1], tile) if q >= j else None for q in js] for j in js]
        for j in js:
            inv = 1.0 / piv[j][j]
            for q in range(j + 1, step):
                f = piv[j][q] * inv
                rows[q] = rows[q] - f * rows[j]
                cols[q] = cols[q] - f[None] * cols[j]
                for r in range(q, step):
                    piv[q][r] = piv[q][r] - f * piv[j][r]
            m = m - jnp.where(row_of > i + j, cols[j], 0.0) * (inv * rows[j])[None]
    m = m.reshape(k, 2 * k)
    pivots = jnp.sum(m[:, :k] * eye, axis=1, keepdims=True)
    return m[:, k:] * (1.0 / jnp.sqrt(pivots))


def finish_body(scale, s_ref, t_ref, q_ref, p_ref):
    k, sk = s_ref.shape
    total = jnp.sum(t_ref[...], axis=0)
    inv = inverse_factor(unfold(total[k:]))
    both = jnp.concatenate([s_ref[...], total[:k] * scale], axis=1)
    both = jnp.dot(inv, both, precision=HI, preferred_element_type=F32)
    q_ref[...] = both[:, :sk]
    p_ref[...] = both[:, sk:]


def call(body, outs, name, *args):
    shapes = [jax.ShapeDtypeStruct(s, F32) for s in outs]
    where = [SMEM if a.ndim == 1 else VMEM for a in args]
    return pl.pallas_call(
        body, out_shape=shapes, in_specs=where, out_specs=[VMEM] * len(outs), compiler_params=BIG, name=name
    )(*args)


def local(sketch, slab):
    k, sk = sketch.shape
    nl, ny, nc, nx = (lax.axis_size(a) for a in ("zl", "y", "c", "x"))
    nh = len(PLACE)
    rows, cols = slab.shape
    ng = nl * ny
    out = cols // (nh * ng * nc)
    at = lax.axis_index("c").astype(jnp.int32)[None]

    (own,) = call(functools.partial(pack_body, 1.0 / (sk * nh * ng * nc * nx)), [(nc * nx, GRAM + SUB, out)], "pack", sketch)
    own = lax.all_to_all(own, ("c", "x"), 0, 0, tiled=True)
    (away,) = call(functools.partial(away_body, out), [(rows, cols // nc)], "away", at, slab)
    away = lax.ppermute(away, "c", [(0, 1), (1, 0)])
    rows *= nc
    (sent,) = call(functools.partial(sort_body, ny), [(ng, nh * rows + rows // 2 + GRAM, out)], "sort", at, slab, away, own)
    sent = lax.all_to_all(sent, ("zl", "y"), 0, 0, tiled=True)
    (part,) = call(functools.partial(project_body, rows), [(nh, k + GRAM, out)], "project", sent)
    part = lax.all_to_all(part, ("z2", "z1", "z0"), 0, 0, tiled=True)
    scale = 1.0 / (rows * nh * ng) ** 0.5
    ortho, projected = call(functools.partial(finish_body, scale), [(k, sk), (k, out)], "finish", sketch, part)
    return ortho, projected


def solution(mesh):
    nx = mesh.shape["narrow"]
    grid = Mesh(mesh.devices.reshape(2, 2, 2, 2, 4, 2, nx), ("z0", "z1", "z2", "zl", "y", "c", "x"))
    wide = ("z0", "z1", "z2", "zl", "y", "c")
    return jax.shard_map(
        local,
        mesh=grid,
        in_specs=(P(None, (*wide, "x")), P(wide, "x")),
        out_specs=(P(None, (*wide, "x")), P(None, ("x", *wide))),
        check_vma=False,
    )
```

```python
import functools

import jax
import jax.numpy as jnp
from jax import lax
from jax.experimental import pallas as pl
from jax.experimental.pallas import tpu as pltpu
from jax.sharding import Mesh, PartitionSpec as P

SUB = 8
HI = lax.Precision.HIGHEST
SMEM = pl.BlockSpec(memory_space=pltpu.SMEM)
VMEM = pl.BlockSpec(memory_space=pltpu.VMEM)
BIG = pltpu.CompilerParams(vmem_limit_bytes=32 * 2**20)
F32 = jnp.float32
PLACE = (0, 4, 2, 6, 1, 5, 3, 7)
GROUP = (0, 1, 2, 3, 4, 5, 6, 7)
NEAR = (0, 2, 4, 6, 1, 3, 5, 7)


GRAM = 24


def fold(gram):
    k = gram.shape[0]
    h, q = k // 2, k // 4
    a, b, c = gram[:h, :h], gram[:h, h:], gram[h:, h:]
    row, col = (lax.broadcasted_iota(jnp.int32, (h, h), d) for d in (0, 1))
    both = jnp.concatenate([jnp.where(row > col, a, c), b], axis=1)
    both = jnp.concatenate([both[:q], both[q:]], axis=1)
    diag = jnp.sum(jnp.where(row == col, a, 0.0), axis=0, keepdims=True)
    diag = jnp.concatenate([diag, jnp.zeros((1, 2 * k - h), F32)], axis=1)
    return jnp.concatenate([both, diag, jnp.zeros((GRAM - q - 1, 2 * k), F32)], axis=0)


def unfold(tile):
    k = tile.shape[1] // 2
    h, q = k // 2, k // 4
    both = jnp.concatenate([tile[:q, :k], tile[:q, k:]], axis=0)
    turned = both.T
    row, col = (lax.broadcasted_iota(jnp.int32, (h, h), d) for d in (0, 1))
    x, xt = both[:, :h], turned[:h]
    diag = jnp.broadcast_to(tile[q : q + 1, :h], (h, h))
    a = jnp.where(row > col, x, jnp.where(row < col, xt, diag))
    c = jnp.where(row <= col, x, xt)
    return jnp.concatenate(
        [jnp.concatenate([a, both[:, h:]], axis=1), jnp.concatenate([turned[h:], c], axis=1)], axis=0
    )


def pack_body(scale, s_ref, o_ref):
    s = s_ref[...]
    gram = lax.dot_general(s, s, (((1,), (1,)), ((), ())), precision=HI, preferred_element_type=F32) * scale
    sel = s.T[:SUB]
    sel = jnp.concatenate([sel, jnp.zeros_like(sel)], axis=1)
    o_ref[...] = jnp.broadcast_to(jnp.concatenate([fold(gram), sel], axis=0)[None], o_ref.shape)


def away_body(w, at_ref, x_ref, o_ref):
    for b in range(o_ref.shape[1] // w):
        col = pl.multiple_of((2 * b + 1 - at_ref[0]) * w, w)
        o_ref[:, b * w : (b + 1) * w] = x_ref[:, pl.ds(col, w)]


def sort_body(at_ref, x_ref, a_ref, t_ref, o_ref):
    ng = o_ref.shape[0]
    rows = x_ref.shape[0]
    _, tall, w = t_ref.shape
    nh = a_ref.shape[1] // (ng * w)
    k = w // 2
    half = tall - SUB
    c = at_ref[0]
    mine = pl.multiple_of(c * rows, rows)
    other = pl.multiple_of((1 - c) * rows, rows)
    for g in range(ng):
        for zh in range(nh):
            b = zh * ng + GROUP[g]
            base = zh * 2 * rows
            o_ref[g, pl.ds(base + mine, rows)] = x_ref[:, pl.ds(pl.multiple_of((2 * b + c) * w, w), w)]
            o_ref[g, pl.ds(base + other, rows)] = a_ref[:, b * w : (b + 1) * w]
    n = t_ref.shape[0]
    sel = [t_ref[p, half:, :k] for p in NEAR]
    sel = jnp.concatenate([jnp.concatenate(sel[: n // 2], axis=0), jnp.concatenate(sel[n // 2 :], axis=0)], axis=1)
    gram = jnp.sum(t_ref[:, :half], axis=0)
    tail = jnp.concatenate([sel, gram], axis=0)
    o_ref[:, nh * 2 * rows :] = jnp.broadcast_to(tail[None], (ng, *tail.shape))


def project_body(rows, t_ref, o_ref):
    ng = t_ref.shape[0]
    nh, tall, w = o_ref.shape
    k = w // 2
    at = nh * rows
    sel = [t_ref[g, at : at + rows // 2, h * k : (h + 1) * k] for g in range(ng) for h in range(2)]
    sel = jnp.concatenate(sel, axis=0)
    step = 2
    for z0 in range(0, nh, step):
        wide = [jnp.concatenate([t_ref[g, z * rows : (z + 1) * rows] for g in range(ng)], axis=0) for z in range(z0, z0 + step)]
        res = lax.dot_general(
            sel, jnp.concatenate(wide, axis=1), (((0,), (0,)), ((), ())), precision=HI, preferred_element_type=F32
        )
        for z in range(step):
            o_ref[PLACE[z0 + z], :k] = res[:, z * w : (z + 1) * w]
    gram = jnp.sum(t_ref[:, at + rows // 2 :], axis=0)
    o_ref[:, k:] = jnp.broadcast_to(gram[None], (nh, tall - k, w))


def inverse_factor(gram):
    k = gram.shape[0]
    eye = (lax.broadcasted_iota(jnp.int32, (k, k), 0) == lax.broadcasted_iota(jnp.int32, (k, k), 1)).astype(F32)
    m = jnp.concatenate([gram, eye], axis=1).reshape(k // SUB, SUB, 2 * k)
    tile = (SUB, 2 * k)
    row_of = lax.broadcasted_iota(jnp.int32, m.shape, 0) * SUB + lax.broadcasted_iota(jnp.int32, m.shape, 1)
    step = SUB
    for i in range(0, k, step):
        js = range(step)
        rows = [jnp.broadcast_to(m[(i + j) // SUB, (i + j) % SUB : (i + j) % SUB + 1], tile) for j in js]
        cols = [jnp.broadcast_to(m[:, :, i + j : i + j + 1], m.shape) for j in js]
        piv = [[jnp.broadcast_to(rows[j][:, i + q : i + q + 1], tile) if q >= j else None for q in js] for j in js]
        for j in js:
            inv = 1.0 / piv[j][j]
            for q in range(j + 1, step):
                f = piv[j][q] * inv
                rows[q] = rows[q] - f * rows[j]
                cols[q] = cols[q] - f[None] * cols[j]
                for r in range(q, step):
                    piv[q][r] = piv[q][r] - f * piv[j][r]
            m = m - jnp.where(row_of > i + j, cols[j], 0.0) * (inv * rows[j])[None]
    m = m.reshape(k, 2 * k)
    pivots = jnp.sum(m[:, :k] * eye, axis=1, keepdims=True)
    return m[:, k:] * (1.0 / jnp.sqrt(pivots))


def finish_body(scale, s_ref, t_ref, q_ref, p_ref):
    k, sk = s_ref.shape
    total = jnp.sum(t_ref[...], axis=0)
    inv = inverse_factor(unfold(total[k:]))
    both = jnp.concatenate([s_ref[...], total[:k] * scale], axis=1)
    both = jnp.dot(inv, both, precision=HI, preferred_element_type=F32)
    q_ref[...] = both[:, :sk]
    p_ref[...] = both[:, sk:]


def call(body, outs, name, *args):
    shapes = [jax.ShapeDtypeStruct(s, F32) for s in outs]
    where = [SMEM if a.ndim == 1 else VMEM for a in args]
    return pl.pallas_call(
        body, out_shape=shapes, in_specs=where, out_specs=[VMEM] * len(outs), compiler_params=BIG, name=name
    )(*args)


def local(sketch, slab):
    k, sk = sketch.shape
    nh, ng, nc, nx = len(PLACE), len(GROUP), 2, 4
    rows, cols = slab.shape
    out = cols // (nh * ng * nc)
    at = lax.axis_index("c").astype(jnp.int32)[None]

    (own,) = call(functools.partial(pack_body, 1.0 / (sk * nh * ng * nc * nx)), [(nc * nx, GRAM + SUB, out)], "pack", sketch)
    own = lax.all_to_all(own, ("x1", "x0", "c"), 0, 0, tiled=True)
    (away,) = call(functools.partial(away_body, out), [(rows, cols // nc)], "away", at, slab)
    away = lax.ppermute(away, "c", [(0, 1), (1, 0)])
    rows *= nc
    (sent,) = call(sort_body, [(ng, nh * rows + rows // 2 + GRAM, out)], "sort", at, slab, away, own)
    sent = lax.all_to_all(sent, ("zl", "y1", "y0"), 0, 0, tiled=True)
    (part,) = call(functools.partial(project_body, rows), [(nh, k + GRAM, out)], "project", sent)
    part = lax.all_to_all(part, ("z2", "z1", "z0"), 0, 0, tiled=True)
    scale = 1.0 / (rows * nh * ng) ** 0.5
    ortho, projected = call(functools.partial(finish_body, scale), [(k, sk), (k, out)], "finish", sketch, part)
    return ortho, projected


def solution(mesh):
    wide, narrow = ("z0", "z1", "z2", "zl", "y1", "y0", "c"), ("x1", "x0")
    grid = Mesh(mesh.devices.reshape((2,) * 9), wide + narrow)
    return jax.shard_map(
        local,
        mesh=grid,
        in_specs=(P(None, wide + narrow), P(wide, narrow)),
        out_specs=(P(None, wide + narrow), P(None, narrow + wide)),
        check_vma=False,
    )
```

```python
import functools

import jax
import jax.numpy as jnp
from jax import lax
from jax.experimental import pallas as pl
from jax.experimental.pallas import tpu as pltpu
from jax.sharding import Mesh, PartitionSpec as P

SUB = 8
HI = lax.Precision.HIGHEST
SMEM = pl.BlockSpec(memory_space=pltpu.SMEM)
VMEM = pl.BlockSpec(memory_space=pltpu.VMEM)
BIG = pltpu.CompilerParams(vmem_limit_bytes=32 * 2**20)
F32 = jnp.float32
PLACE = (0, 4, 2, 6, 1, 5, 3, 7)
GROUP = (0, 2, 1, 3, 4, 6, 5, 7)
NEAR = (0, 2, 4, 6, 1, 3, 5, 7)


GRAM = 24


def fold(gram):
    k = gram.shape[0]
    h, q = k // 2, k // 4
    a, b, c = gram[:h, :h], gram[:h, h:], gram[h:, h:]
    row, col = (lax.broadcasted_iota(jnp.int32, (h, h), d) for d in (0, 1))
    both = jnp.concatenate([jnp.where(row > col, a, c), b], axis=1)
    both = jnp.concatenate([both[:q], both[q:]], axis=1)
    diag = jnp.sum(jnp.where(row == col, a, 0.0), axis=0, keepdims=True)
    diag = jnp.concatenate([diag, jnp.zeros((1, 2 * k - h), F32)], axis=1)
    return jnp.concatenate([both, diag, jnp.zeros((GRAM - q - 1, 2 * k), F32)], axis=0)


def unfold(tile):
    k = tile.shape[1] // 2
    h, q = k // 2, k // 4
    both = jnp.concatenate([tile[:q, :k], tile[:q, k:]], axis=0)
    turned = both.T
    row, col = (lax.broadcasted_iota(jnp.int32, (h, h), d) for d in (0, 1))
    x, xt = both[:, :h], turned[:h]
    diag = jnp.broadcast_to(tile[q : q + 1, :h], (h, h))
    a = jnp.where(row > col, x, jnp.where(row < col, xt, diag))
    c = jnp.where(row <= col, x, xt)
    return jnp.concatenate(
        [jnp.concatenate([a, both[:, h:]], axis=1), jnp.concatenate([turned[h:], c], axis=1)], axis=0
    )


def pack_body(scale, s_ref, o_ref):
    s = s_ref[...]
    gram = lax.dot_general(s, s, (((1,), (1,)), ((), ())), precision=HI, preferred_element_type=F32) * scale
    sel = s.T[:SUB]
    sel = jnp.concatenate([sel, jnp.zeros_like(sel)], axis=1)
    o_ref[...] = jnp.broadcast_to(jnp.concatenate([fold(gram), sel], axis=0)[None], o_ref.shape)


def away_body(w, at_ref, x_ref, o_ref):
    for b in range(o_ref.shape[1] // w):
        col = pl.multiple_of((2 * b + 1 - at_ref[0]) * w, w)
        o_ref[:, b * w : (b + 1) * w] = x_ref[:, pl.ds(col, w)]


def sort_body(at_ref, x_ref, a_ref, t_ref, o_ref):
    ng = o_ref.shape[0]
    rows = x_ref.shape[0]
    _, tall, w = t_ref.shape
    nh = a_ref.shape[1] // (ng * w)
    k = w // 2
    half = tall - SUB
    c = at_ref[0]
    mine = pl.multiple_of(c * rows, rows)
    other = pl.multiple_of((1 - c) * rows, rows)
    for g in range(ng):
        for zh in range(nh):
            b = zh * ng + GROUP[g]
            base = zh * 2 * rows
            o_ref[g, pl.ds(base + mine, rows)] = x_ref[:, pl.ds(pl.multiple_of((2 * b + c) * w, w), w)]
            o_ref[g, pl.ds(base + other, rows)] = a_ref[:, b * w : (b + 1) * w]
    n = t_ref.shape[0]
    sel = [t_ref[p, half:, :k] for p in NEAR]
    sel = jnp.concatenate([jnp.concatenate(sel[: n // 2], axis=0), jnp.concatenate(sel[n // 2 :], axis=0)], axis=1)
    gram = jnp.sum(t_ref[:, :half], axis=0)
    tail = jnp.concatenate([sel, gram], axis=0)
    o_ref[:, nh * 2 * rows :] = jnp.broadcast_to(tail[None], (ng, *tail.shape))


def project_body(rows, t_ref, o_ref):
    ng = t_ref.shape[0]
    nh, tall, w = o_ref.shape
    k = w // 2
    at = nh * rows
    sel = [t_ref[g, at : at + rows // 2, h * k : (h + 1) * k] for g in range(ng) for h in range(2)]
    sel = jnp.concatenate(sel, axis=0)
    step = 2
    for z0 in range(0, nh, step):
        wide = [jnp.concatenate([t_ref[g, z * rows : (z + 1) * rows] for g in range(ng)], axis=0) for z in range(z0, z0 + step)]
        res = lax.dot_general(
            sel, jnp.concatenate(wide, axis=1), (((0,), (0,)), ((), ())), precision=HI, preferred_element_type=F32
        )
        for z in range(step):
            o_ref[PLACE[z0 + z], :k] = res[:, z * w : (z + 1) * w]
    gram = jnp.sum(t_ref[:, at + rows // 2 :], axis=0)
    o_ref[:, k:] = jnp.broadcast_to(gram[None], (nh, tall - k, w))


def inverse_factor(gram):
    k = gram.shape[0]
    eye = (lax.broadcasted_iota(jnp.int32, (k, k), 0) == lax.broadcasted_iota(jnp.int32, (k, k), 1)).astype(F32)
    m = jnp.concatenate([gram, eye], axis=1).reshape(k // SUB, SUB, 2 * k)
    tile = (SUB, 2 * k)
    row_of = lax.broadcasted_iota(jnp.int32, m.shape, 0) * SUB + lax.broadcasted_iota(jnp.int32, m.shape, 1)
    step = SUB
    for i in range(0, k, step):
        js = range(step)
        rows = [jnp.broadcast_to(m[(i + j) // SUB, (i + j) % SUB : (i + j) % SUB + 1], tile) for j in js]
        cols = [jnp.broadcast_to(m[:, :, i + j : i + j + 1], m.shape) for j in js]
        piv = [[jnp.broadcast_to(rows[j][:, i + q : i + q + 1], tile) if q >= j else None for q in js] for j in js]
        for j in js:
            inv = 1.0 / piv[j][j]
            for q in range(j + 1, step):
                f = piv[j][q] * inv
                rows[q] = rows[q] - f * rows[j]
                cols[q] = cols[q] - f[None] * cols[j]
                for r in range(q, step):
                    piv[q][r] = piv[q][r] - f * piv[j][r]
            m = m - jnp.where(row_of > i + j, cols[j], 0.0) * (inv * rows[j])[None]
    m = m.reshape(k, 2 * k)
    pivots = jnp.sum(m[:, :k] * eye, axis=1, keepdims=True)
    return m[:, k:] * (1.0 / jnp.sqrt(pivots))


def finish_body(scale, s_ref, t_ref, q_ref, p_ref):
    k, sk = s_ref.shape
    total = jnp.sum(t_ref[...], axis=0)
    inv = inverse_factor(unfold(total[k:]))
    both = jnp.concatenate([s_ref[...], total[:k] * scale], axis=1)
    both = jnp.dot(inv, both, precision=HI, preferred_element_type=F32)
    q_ref[...] = both[:, :sk]
    p_ref[...] = both[:, sk:]


def call(body, outs, name, *args):
    shapes = [jax.ShapeDtypeStruct(s, F32) for s in outs]
    where = [SMEM if a.ndim == 1 else VMEM for a in args]
    return pl.pallas_call(
        body, out_shape=shapes, in_specs=where, out_specs=[VMEM] * len(outs), compiler_params=BIG, name=name
    )(*args)


def local(sketch, slab):
    k, sk = sketch.shape
    nh, ng, nc, nx = len(PLACE), len(GROUP), 2, 4
    rows, cols = slab.shape
    out = cols // (nh * ng * nc)
    at = lax.axis_index("c").astype(jnp.int32)[None]

    (own,) = call(functools.partial(pack_body, 1.0 / (sk * nh * ng * nc * nx)), [(nc * nx, GRAM + SUB, out)], "pack", sketch)
    own = lax.all_to_all(own, ("x1", "x0", "c"), 0, 0, tiled=True)
    (away,) = call(functools.partial(away_body, out), [(rows, cols // nc)], "away", at, slab)
    away = lax.ppermute(away, "c", [(0, 1), (1, 0)])
    rows *= nc
    (sent,) = call(sort_body, [(ng, nh * rows + rows // 2 + GRAM, out)], "sort", at, slab, away, own)
    sent = lax.all_to_all(sent, ("zl", "y0", "y1"), 0, 0, tiled=True)
    (part,) = call(functools.partial(project_body, rows), [(nh, k + GRAM, out)], "project", sent)
    part = lax.all_to_all(part, ("z2", "z1", "z0"), 0, 0, tiled=True)
    scale = 1.0 / (rows * nh * ng) ** 0.5
    ortho, projected = call(functools.partial(finish_body, scale), [(k, sk), (k, out)], "finish", sketch, part)
    return ortho, projected


def solution(mesh):
    wide, narrow = ("z0", "z1", "z2", "zl", "y1", "y0", "c"), ("x1", "x0")
    grid = Mesh(mesh.devices.reshape((2,) * 9), wide + narrow)
    return jax.shard_map(
        local,
        mesh=grid,
        in_specs=(P(None, wide + narrow), P(wide, narrow)),
        out_specs=(P(None, wide + narrow), P(None, narrow + wide)),
        check_vma=False,
    )
```
